32 devices in a mesh: seq: 4 (over z), exp: 8 (over y, x, core).
Axes of the slice: x: 2, y: 2, z: 4, core: 2. Of those that a mesh axis runs over, the one named last changes fastest.
Arguments:
- hidden: bfloat16 [8, 1024, 768], P('exp', 'seq'), may hold values from -40 to 40
- ssm_input: bfloat16 [8, 1024, 1536], P('exp', 'seq'), may hold values from -6 to 6
- ssm_gate: bfloat16 [8, 1024, 1536], P('exp', 'seq'), may hold values from -6 to 6
- write_proj: bfloat16 [8, 1024, 128], P('exp', 'seq'), may hold values from -1 to 1
- read_proj: bfloat16 [8, 1024, 128], P('exp', 'seq'), may hold values from -1 to 1
- dt_raw: float32 [8, 24, 1024], P('exp', None, 'seq'), may hold values from -4.5 to 150
- dt_bias: float32 [24], replicated, may hold values from -2 to -0.5
- a_log: float32 [24], replicated, may hold values from -7 to -1.2
- d_skip: float32 [24], replicated, may hold values from 0.5 to 2
- norm_gain: float32 [1536], replicated, may hold values from 0.25 to 1.75
- out_weight: bfloat16 [1536, 768], replicated, may hold values from -0.15625 to 0.15625
- moe_gain: float32 [768], replicated, may hold values from 0.25 to 1.75
- expert_ids: int32 [8, 1024, 2], P('exp', 'seq'), may hold values from 0 to 7, all different within a row; in each aligned block of 256 rows (0 to 255, 256 to 511, ..., all dimensions but the last counted through in order) at most 96 rows name the same one
- gate_values: float32 [8, 1024, 2], P('exp', 'seq'), may hold values from 0.2 to 1
- w_gate: bfloat16 [8, 768, 1536], P('exp'), may hold values from -0.21875 to 0.21875
- w_up: bfloat16 [8, 768, 1536], P('exp'), may hold values from -0.21875 to 0.21875
- w_down: bfloat16 [8, 1536, 768], P('exp'), may hold values from -0.15625 to 0.15625
Outputs:
- layer_out: bfloat16 [8, 1024, 768], P('exp', 'seq')
The draws below stay inside these ranges and needn't reach their ends.
Inputs may be any that keep to these rules, and one draw needn't show every extreme that they name: `expert_ids`: the two experts of a position differ. In each block of 256 positions of one trace (the rows of one device) no expert is named by more than 96 of the block's positions, a bound that some block reaches.
All inputs are finite; a program needn't handle non-finite values.
Results may differ from the reference program's by a relative error of at most 0.005.
Values may be sent and summed in bfloat16 or wider, within the bound.
No kernel may reach another device: no remote copies, remote signals or barrier semaphores. Data moves between devices by JAX's collectives and lax.ppermute only.
A program may use at most 64 MiB of HBM per device.

```python
import math
import jax
import jax.numpy as jnp
import numpy as np
from jax import lax

D_MODEL = 768
HEADS = 24
STATE = 128
FF = 1536
SEQ_DEV = 256
EXPERTS = 8
TRACES = 8
RECORD_SPAN = 1024
INNER = 1536
CAP = 96
N_SEQ = 4


def draw_hidden(key, part):
    shape = (TRACES, RECORD_SPAN, D_MODEL)
    key_base, key_rows, key_cols = jax.random.split(key, 3)
    row_scale = jnp.exp(jax.random.uniform(key_rows, (TRACES, RECORD_SPAN, 1), jnp.float32, math.log(0.3), math.log(3.0)))
    col_scale = jnp.exp(jax.random.uniform(key_cols, (1, 1, D_MODEL), jnp.float32, math.log(0.3), math.log(3.0)))
    base = jnp.clip(jax.random.normal(key_base, shape, jnp.float32), -4.0, 4.0)
    return (base * row_scale * col_scale).astype(jnp.bfloat16)


def draw_dt_raw(key, part):
    key_noise, key_offset, key_where, seed_tile_span = jax.random.split(key, 4)
    shape = (TRACES, HEADS, RECORD_SPAN)
    jitter_draw = jnp.clip(0.7 * jax.random.normal(key_noise, shape, jnp.float32), -3.0, 3.0)
    block_count = RECORD_SPAN // SEQ_DEV
    opening_shift = jax.random.uniform(key_offset, (TRACES, 1, block_count), jnp.float32, -1.0, 1.0)
    opening_shift = jnp.repeat(opening_shift, SEQ_DEV, axis=2)
    record_locations = jax.random.randint(key_where, (TRACES, 3), 0, RECORD_SPAN)
    fetch_groups = jnp.any(jnp.arange(RECORD_SPAN)[None, None, :] == record_locations[:, :, None], axis=1)[:, None, :]
    tile_rows_count = jax.random.uniform(seed_tile_span, (TRACES, 1, RECORD_SPAN), jnp.float32, 60.0, 150.0)
    return jnp.where(fetch_groups, tile_rows_count, jitter_draw + opening_shift)


def draw_a_log(key, part):
    key_fast, key_slow, key_pick = jax.random.split(key, 3)
    slow_rates = jax.random.uniform(key_slow, (HEADS,), jnp.float32, math.log(0.001), math.log(0.003))
    fast_rates = jax.random.uniform(key_fast, (HEADS,), jnp.float32, math.log(0.1), math.log(0.3))
    chosen = jax.random.uniform(key_pick, (HEADS,), jnp.float32) < 0.5
    return jnp.where(chosen, fast_rates, slow_rates)


def levels(own_key, extent, cuts, least, top_value):
    factor_of, own = 1.0, jax.random.fold_in(own_key, 6)
    for position, shards_of in cuts:
        heights = jnp.exp(jax.random.uniform(jax.random.fold_in(own, position), (shards_of,), jnp.float32, least / len(cuts), top_value / len(cuts)))
        factor_of = factor_of * jnp.repeat(heights, extent[position] // shards_of).reshape([-1 if axis == position else 1 for axis in range(len(extent))])
    return factor_of


def deal_out(stream_key, own, number, rows, count, top, most, skew):
    sequence = jax.random.permutation(stream_key, count)
    packed, usual = load_shares(count, rows * top, most, skew, True), load_shares(count, rows * top, most, skew, False)
    places = jnp.arange(count)

    def named(tallies, offset_by):
        used = int((tallies > 0).sum())
        fixed = max(1, used // 4)
        passed = fixed + (places - fixed + offset_by * (used - fixed)) % max(1, count - fixed)
        return jnp.zeros((count,), jnp.int32).at[sequence[jnp.where(places < fixed, places, passed)]].set(jnp.asarray(tallies, jnp.int32))

    tallies = jnp.where(number % 4 == 0, named(packed, number // 4), named(usual, number - number // 4 - 1))
    mixed = jax.random.permutation(jax.random.fold_in(own, 3), count)
    source_of, taker = mixed[0:count // 2 * 2:2], mixed[1:count // 2 * 2:2]
    slack = jnp.minimum(tallies[source_of] - 1, most - tallies[taker]) // 2
    slack = jnp.where((source_of == sequence[0]) | (taker == sequence[0]) | (tallies[taker] == 0), 0, jnp.maximum(slack, 0))
    passed = jax.random.randint(jax.random.fold_in(own, 4), (count // 2,), 0, 1 << 20) % (slack + 1)
    tallies = tallies.at[source_of].add(-passed).at[taker].add(passed)
    members = jnp.searchsorted(jnp.cumsum(tallies), jnp.arange(rows * top), side="right").astype(jnp.int32)
    table = members.reshape(top, rows).T
    table = table[jax.random.permutation(jax.random.fold_in(own, 1), rows)]
    offset_by = jax.random.randint(jax.random.fold_in(own, 2), (rows, 1), 0, top)
    return jnp.take_along_axis(table, (jnp.arange(top)[None, :] + offset_by) % top, axis=1)


def load_shares(count, total, limit, lean, full):
    loads = [(1 << 20) // math.isqrt(standing ** lean) + 1 for standing in range(1, count + 1)]
    largest = limit if full else min(limit, max(-(-total // count), total * loads[0] // sum(loads)))
    least = 1 if total - largest >= count - 1 else 0
    holding, surplus = [largest] + [least] * (count - 1), total - largest - least * (count - 1)
    while surplus > 0:
        movable = [i for i in range(1, count) if holding[i] < largest] or [i for i in range(1, count) if holding[i] < limit]
        whole, budget = sum([loads[i] for i in movable]), surplus
        for i in movable:
            addition = min(limit - holding[i], max(1, budget * loads[i] // whole), surplus)
            holding[i] = holding[i] + addition
            surplus = surplus - addition
    return np.array(holding)


def noise(stream_key, dims, width, bound, cuts=(), kind=jnp.bfloat16):
    factor_of = levels(stream_key, dims, cuts, -0.22, 0.18) if cuts else 1.0
    entries = jax.random.normal(stream_key, dims, jnp.float32) * width * factor_of
    return jnp.minimum(jnp.maximum(entries, -bound), bound).astype(kind)


def setup_inputs(seed: int = 0) -> dict:
    arg_keys = jax.random.split(jax.random.key(seed), 18)
    hidden = draw_hidden(jax.random.fold_in(arg_keys[17], 71), 0)
    ssm_input = noise(arg_keys[1], (TRACES, RECORD_SPAN, INNER), 1.0, 6.0, ((0, 8), (1, 4)))
    ssm_gate = noise(arg_keys[2], (TRACES, RECORD_SPAN, INNER), 1.0, 6.0, ((0, 8), (1, 4)))
    write_proj = noise(arg_keys[3], (TRACES, RECORD_SPAN, STATE), 0.16, 1.0, ((0, 8), (1, 4)))
    read_proj = noise(arg_keys[4], (TRACES, RECORD_SPAN, STATE), 0.16, 1.0, ((0, 8), (1, 4)))
    dt_raw = draw_dt_raw(jax.random.fold_in(arg_keys[17], 71), 0)
    dt_bias = jnp.clip(jax.random.uniform(arg_keys[6], (HEADS,), jnp.float32, -2.0, -0.5), -2.0, -0.5)
    a_log = draw_a_log(jax.random.fold_in(arg_keys[17], 71), 0)
    d_skip = jnp.clip(jax.random.uniform(arg_keys[8], (HEADS,), jnp.float32, 0.5, 2.0), 0.5, 2.0)
    norm_gain = jnp.clip(1.0 + 0.15 * jax.random.normal(arg_keys[9], (INNER,), jnp.float32), 0.25, 1.75)
    out_weight = noise(arg_keys[10], (INNER, D_MODEL), INNER ** -0.5, 0.15625)
    moe_gain = jnp.clip(1.0 + 0.15 * jax.random.normal(arg_keys[11], (D_MODEL,), jnp.float32), 0.25, 1.75)
    expert_ids_keys = jax.random.split(jax.random.fold_in(arg_keys[12], 1), TRACES * RECORD_SPAN // SEQ_DEV)
    expert_ids_turns = jax.random.permutation(jax.random.fold_in(arg_keys[12], 3), TRACES * RECORD_SPAN // SEQ_DEV)
    expert_ids = jax.vmap(lambda own, number: deal_out(jax.random.fold_in(arg_keys[12], 2), own, number, SEQ_DEV, EXPERTS, 2, CAP, 1))(expert_ids_keys, expert_ids_turns).reshape((TRACES, RECORD_SPAN, 2))
    gate_values = jnp.clip(0.2 + 0.8 * jax.random.uniform(arg_keys[13], (TRACES, RECORD_SPAN, 2), jnp.float32) ** levels(arg_keys[13], (TRACES, RECORD_SPAN, 2), ((0, 8), (1, 4)), -0.2, 0.2), 0.2, 1.0)
    w_gate = noise(arg_keys[14], (EXPERTS, D_MODEL, FF), D_MODEL ** -0.5, 0.21875, ((0, 8),))
    w_up = noise(arg_keys[15], (EXPERTS, D_MODEL, FF), D_MODEL ** -0.5, 0.21875, ((0, 8),))
    w_down = noise(arg_keys[16], (EXPERTS, FF, D_MODEL), FF ** -0.5, 0.15625, ((0, 8),))
    return dict(hidden=hidden, ssm_input=ssm_input, ssm_gate=ssm_gate, write_proj=write_proj, read_proj=read_proj, dt_raw=dt_raw, dt_bias=dt_bias, a_log=a_log, d_skip=d_skip, norm_gain=norm_gain, out_weight=out_weight, moe_gain=moe_gain, expert_ids=expert_ids, gate_values=gate_values, w_gate=w_gate, w_up=w_up, w_down=w_down)


EPS = 1e-05

def local_block(signal, write_rows, read_rows, raw_steps, dt_bias, a_log):
    positions = signal.shape[0]
    head_count = raw_steps.shape[0]
    step_size = jax.nn.softplus(raw_steps + dt_bias[:, None])
    log_decay = -jnp.exp(a_log)[:, None] * step_size
    cumulative = jnp.cumsum(log_decay, axis=1)
    scores = jnp.dot(read_rows, write_rows.T, preferred_element_type=jnp.float32)
    causal = jnp.arange(positions)[:, None] >= jnp.arange(positions)[None, :]
    spread = cumulative[:, :, None] - cumulative[:, None, :]
    kernel = jnp.where(causal[None], jnp.exp(jnp.where(causal[None], spread, 0.0)), 0.0)
    weights = lax.optimization_barrier((scores[None] * kernel * step_size[:, None, :]).astype(jnp.bfloat16))
    signal_heads = signal.reshape(positions, head_count, -1).astype(jnp.float32)
    y_intra = jnp.einsum('hts,shp->thp', weights.astype(jnp.float32), signal_heads)
    to_end = jnp.exp(cumulative[:, -1:] - cumulative) * step_size
    scaled = lax.optimization_barrier((signal_heads * to_end.T[:, :, None]).astype(jnp.bfloat16))
    block_state = jnp.einsum('shp,sn->hpn', scaled.astype(jnp.float32), write_rows.astype(jnp.float32))
    return (y_intra, block_state, jnp.exp(cumulative[:, -1]), cumulative)

def finish(y_intra, cumulative, read_rows, incoming, signal, gate_rows, d_skip, norm_gain):
    positions = signal.shape[0]
    signal_heads = signal.reshape(positions, d_skip.shape[0], -1).astype(jnp.float32)
    carried = jnp.einsum('tn,hpn->thp', read_rows.astype(jnp.float32), incoming, precision=lax.Precision.HIGHEST)
    mixed = y_intra + jnp.exp(cumulative).T[:, :, None] * carried + d_skip[None, :, None] * signal_heads
    mixed = mixed.reshape(positions, -1) * jax.nn.silu(gate_rows.astype(jnp.float32))
    scale = lax.rsqrt(lax.optimization_barrier(jnp.mean(mixed * mixed, axis=-1, keepdims=True)) + EPS)
    return (mixed * scale * norm_gain).astype(jnp.bfloat16)

def slot_targets(expert_rows, experts, capacity):
    flat_ids = expert_rows.reshape(-1)
    hits = (flat_ids[:, None] == jnp.arange(experts, dtype=jnp.int32)[None, :]).astype(jnp.int32)
    before = jnp.cumsum(hits, axis=0) - hits
    slot = lax.optimization_barrier(jnp.sum(before * hits, axis=1, dtype=jnp.int32)).reshape(expert_rows.shape)
    return (expert_rows * capacity + slot).astype(jnp.int32)

def reference(hidden, ssm_input, ssm_gate, write_proj, read_proj, dt_raw, dt_bias, a_log, d_skip, norm_gain, out_weight, moe_gain, expert_ids, gate_values, w_gate, w_up, w_down):
    gate_wide = w_gate.astype(jnp.float32)
    up_wide = w_up.astype(jnp.float32)
    down_wide = w_down.astype(jnp.float32)

    def one_trace(pieces):
        hid, signal, gate_rows, write_rows, read_rows, raw_steps, id_rows, gate_weights = pieces
        signal_b = signal.reshape(N_SEQ, SEQ_DEV, -1)
        gate_b = gate_rows.reshape(N_SEQ, SEQ_DEV, -1)
        write_b = write_rows.reshape(N_SEQ, SEQ_DEV, -1)
        read_b = read_rows.reshape(N_SEQ, SEQ_DEV, -1)
        raw_b = raw_steps.reshape(raw_steps.shape[0], N_SEQ, SEQ_DEV).transpose(1, 0, 2)
        y_intra, hidden_memory, decays, cumul = jax.vmap(local_block, in_axes=(0, 0, 0, 0, None, None))(signal_b, write_b, read_b, raw_b, dt_bias, a_log)

        def advance(carry_state, inputs):
            block_decay, block_state = inputs
            return (block_decay[:, None, None] * carry_state + block_state, carry_state)
        _, incoming = lax.scan(advance, jnp.zeros_like(hidden_memory[0]), (decays, hidden_memory))
        gated = jax.vmap(finish, in_axes=(0, 0, 0, 0, 0, 0, None, None))(y_intra, cumul, read_b, incoming, signal_b, gate_b, d_skip, norm_gain)
        stream = hid.astype(jnp.float32) + jnp.dot(gated.reshape(RECORD_SPAN, -1), out_weight, preferred_element_type=jnp.float32)
        normed = (stream * lax.rsqrt(lax.optimization_barrier(jnp.mean(stream * stream, axis=-1, keepdims=True)) + EPS) * moe_gain).astype(jnp.bfloat16)
        normed = lax.optimization_barrier(normed)
        targets = jax.vmap(slot_targets, in_axes=(0, None, None))(id_rows.reshape(N_SEQ, SEQ_DEV, 2), EXPERTS, CAP)

        def place(target, rows):
            empty = jnp.zeros((EXPERTS * CAP, D_MODEL), jnp.bfloat16)
            return empty.at[target.reshape(-1)].set(jnp.repeat(rows, 2, axis=0))
        buffers = jax.vmap(place)(targets, normed.reshape(N_SEQ, SEQ_DEV, D_MODEL))
        grouped = buffers.reshape(N_SEQ, EXPERTS, CAP, D_MODEL).transpose(1, 0, 2, 3).reshape(EXPERTS, N_SEQ * CAP, D_MODEL).astype(jnp.float32)
        gate_portion = jnp.einsum('erd,edf->erf', grouped, gate_wide)
        up_part = jnp.einsum('erd,edf->erf', grouped, up_wide)
        active = lax.optimization_barrier((jax.nn.silu(gate_portion) * up_part).astype(jnp.bfloat16))
        out_rows = jnp.einsum('erf,efd->erd', active.astype(jnp.float32), down_wide).astype(jnp.bfloat16)
        back = out_rows.reshape(EXPERTS, N_SEQ, CAP, D_MODEL).transpose(1, 0, 2, 3).reshape(N_SEQ, EXPERTS * CAP, D_MODEL)

        def pick_rows(rows, target):
            return rows[target]
        picked = jax.vmap(pick_rows)(back, targets).reshape(RECORD_SPAN, 2, D_MODEL).astype(jnp.float32)
        total = stream + gate_weights[:, 0:1] * picked[:, 0] + gate_weights[:, 1:2] * picked[:, 1]
        return total.astype(jnp.bfloat16)
    return lax.map(one_trace, (hidden, ssm_input, ssm_gate, write_proj, read_proj, dt_raw, expert_ids, gate_values))
```

```python
import functools

import jax
import jax.numpy as jnp
from jax import lax
from jax.experimental import pallas as pl
from jax.experimental.pallas import tpu as pltpu
from jax.sharding import PartitionSpec as P

EPS = 1e-05
F32 = jnp.float32
BF16 = jnp.bfloat16
CHUNKS = 3


def call(body, name, out_shape, flops, nbytes, **kwargs):
    return pl.pallas_call(
        body,
        out_shape=out_shape,
        name=name,
        compiler_params=pltpu.CompilerParams(vmem_limit_bytes=32 * 2**20),
        cost_estimate=pl.CostEstimate(flops=flops, bytes_accessed=nbytes, transcendentals=0),
        **kwargs,
    )


def dot(a, b):
    return jnp.dot(a, b, preferred_element_type=F32)


def dot_rows(a, b):
    return lax.dot_general(a, b, (((0,), (0,)), ((), ())), preferred_element_type=F32)


def pieces(value, count):
    parts = []
    for _ in range(count):
        part = value.astype(BF16)
        parts.append(part)
        value = value - part.astype(F32)
    return parts


def iota(shape, dim):
    return lax.broadcasted_iota(jnp.int32, shape, dim)


def state_kernel(dt_ref, bias_ref, alog_ref, x_ref, write_ref, cum_ref, step_ref, decay_ref, *state_refs):
    length, inner = x_ref.shape
    heads = dt_ref.shape[0]
    raw = dt_ref[...].T + bias_ref[...]
    step = jnp.maximum(raw, 0.0) + jnp.log1p(jnp.exp(-jnp.abs(raw)))
    log_decay = -jnp.exp(alog_ref[...]) * step
    lower = (iota((length, length), 0) >= iota((length, length), 1)).astype(F32).astype(BF16)
    cum = sum(dot(lower, part) for part in pieces(log_decay, 3))
    last = cum[length - 1 : length, :]
    to_end = jnp.exp(jnp.minimum(last - cum, 0.0)) * step
    expand = (iota((heads, inner), 1) // (inner // heads) == iota((heads, inner), 0)).astype(F32).astype(BF16)
    decay = sum(dot(part, expand) for part in pieces(jnp.broadcast_to(jnp.exp(last), (8, heads)), 3))
    cum_ref[...] = cum
    step_ref[...] = step
    decay_ref[...] = decay[0:1, :]
    ends = pieces(to_end, 2)
    width = inner // len(state_refs)
    for k, state_ref in enumerate(state_refs):
        cols = slice(k * width, (k + 1) * width)
        wide = sum(dot(part, expand[:, cols]) for part in ends)
        scaled = (x_ref[:, cols].astype(F32) * wide).astype(BF16)
        state_ref[...] = dot_rows(write_ref[...], scaled).astype(BF16)


def intra_kernel(xor, capacity, cum_ref, step_ref, x_ref, gate_ref, write_ref, read_ref, skip_ref, ids_ref,
                 own_ref, factor_ref, route_ref, target_ref):
    length, inner = x_ref.shape
    heads = cum_ref.shape[1]
    half = length // 2
    cum = cum_ref[...]
    cum_rows = cum.T
    step_rows = step_ref[...].T
    scores = lax.dot_general(
        read_ref[...], write_ref[...], (((1,), (1,)), ((), ())), preferred_element_type=F32
    )
    scores = jnp.where(iota((length, length), 0) >= iota((length, length), 1), scores, 0.0)
    lanes = 2 * (inner // heads)
    first = iota((length, lanes), 1) < lanes // 2
    first_row = iota((1, lanes), 1) < lanes // 2
    for pair in range(heads // 2):
        cols = slice(pair * lanes, (pair + 1) * lanes)
        x = x_ref[:, cols]
        wide = x.astype(F32)
        masked = [jnp.where(first, wide, 0.0).astype(BF16), jnp.where(first, 0.0, wide).astype(BF16)]
        tops, bottoms = [], []
        for h in (2 * pair, 2 * pair + 1):
            here = cum[:, h : h + 1]
            there = cum_rows[h : h + 1, :]
            steps = step_rows[h : h + 1, :]
            top = jnp.exp(jnp.minimum(here[:half] - there[:, :half], 0.0))
            tops.append((scores[:half, :half] * top * steps[:, :half]).astype(BF16))
            bottom = jnp.exp(jnp.minimum(here[half:] - there, 0.0))
            bottoms.append((scores[half:, :] * bottom * steps).astype(BF16))
        y_top = dot(jnp.concatenate(tops, 1), jnp.concatenate([m[:half] for m in masked], 0))
        y_bottom = dot(jnp.concatenate(bottoms, 1), jnp.concatenate(masked, 0))
        y = jnp.concatenate([y_top, y_bottom], 0)
        skip = jnp.where(first_row, skip_ref[:, 2 * pair : 2 * pair + 1], skip_ref[:, 2 * pair + 1 : 2 * pair + 2])
        gate = gate_ref[:, cols].astype(F32)
        gate = gate / (1.0 + jnp.exp(-gate))
        grown = jnp.exp(jnp.where(first, cum[:, 2 * pair : 2 * pair + 1], cum[:, 2 * pair + 1 : 2 * pair + 2]))
        own_ref[:, cols] = (y + skip * wide) * gate
        factor_ref[:, cols] = grown * gate
    ids = ids_ref[...]
    lane = iota((length, 128), 1)
    hits = [(ids[:, k : k + 1] == lane).astype(F32) for k in range(2)]
    earlier = (iota((length, length), 0) > iota((length, length), 1)).astype(F32).astype(BF16)
    before = dot(earlier, (hits[0] + hits[1]).astype(BF16))
    if xor:
        ids = ids ^ lax.axis_index("exp")
    slots = route_ref.shape[0]
    rows = jnp.zeros((length, slots), F32)
    for k in range(2):
        slot = jnp.sum(before * hits[k], axis=1, keepdims=True).astype(jnp.int32)
        target = ids[:, k : k + 1] * capacity + slot
        target_ref[:, k : k + 1] = target
        rows = jnp.where(target == iota((length, slots), 1), 1.0, rows)
    route_ref[...] = rows.T.astype(BF16)


def mix_kernel(chunks, *refs):
    earlier, latest = refs[:chunks], refs[chunks : 2 * chunks]
    (read_ref, own_ref, factor_ref, norm_ref, weight_ref, hidden_ref, gain_ref, route_ref) = refs[2 * chunks : 2 * chunks + 8]
    stream_ref, *buffer_refs, mixed_ref = refs[2 * chunks + 8 :]
    inner = own_ref.shape[1]
    width = inner // chunks
    total = 0.0
    for k in range(chunks):
        cols = slice(k * width, (k + 1) * width)
        incoming = (earlier[k][...].astype(F32) + latest[k][...].astype(F32)).astype(BF16)
        value = own_ref[:, cols] + factor_ref[:, cols] * dot(read_ref[...], incoming)
        mixed_ref[:, cols] = value
        total = total + jnp.sum(value * value, axis=1, keepdims=True)
    scale = lax.rsqrt(total / inner + EPS)
    gated = (mixed_ref[...] * scale * norm_ref[...]).astype(BF16)
    stream = hidden_ref[...].astype(F32) + dot(gated, weight_ref[...])
    stream_ref[...] = stream
    scale = lax.rsqrt(jnp.mean(stream * stream, axis=1, keepdims=True) + EPS)
    normed = (stream * scale * gain_ref[...]).astype(BF16)
    at = 0
    for buffer_ref in buffer_refs:
        rows = buffer_ref.shape[0]
        buffer_ref[...] = dot(route_ref[at : at + rows, :], normed).astype(BF16)
        at += rows


def expert_kernel(count, *refs):
    rows, (gate_ref, up_ref, down_ref) = refs[:count], refs[count : count + 3]
    outs, total = refs[count + 3 : 2 * count + 3], refs[2 * count + 3]
    x = jnp.concatenate([r[...] for r in rows], 0)
    gate = dot(x, gate_ref[...])
    active = (gate / (1.0 + jnp.exp(-gate)) * dot(x, up_ref[...])).astype(BF16)
    part = dot(active, down_ref[...])
    step, last = pl.program_id(0), pl.num_programs(0) - 1

    @pl.when(step == 0)
    def _():
        total[...] = part

    @pl.when(step > 0)
    def _():
        total[...] += part

    @pl.when(step == last)
    def _():
        at = 0
        for out in outs:
            out[...] = total[at : at + out.shape[0], :].astype(BF16)
            at += out.shape[0]


def run_expert(rows, w_gate, w_up, w_down):
    count, (width, hidden) = len(rows), w_gate.shape
    tile = hidden // 3
    sizes = [r.shape[0] for r in rows]
    row_specs = [pl.BlockSpec((n, width), lambda j: (0, 0)) for n in sizes]
    return call(
        functools.partial(expert_kernel, count),
        "experts",
        [jax.ShapeDtypeStruct((n, width), BF16) for n in sizes],
        6 * sum(sizes) * width * hidden,
        6 * width * hidden + 4 * sum(sizes) * width,
        grid=(hidden // tile,),
        in_specs=row_specs
        + [pl.BlockSpec((width, tile), lambda j: (0, j))] * 2
        + [pl.BlockSpec((tile, width), lambda j: (j, 0))],
        out_specs=row_specs,
        scratch_shapes=[pltpu.VMEM((sum(sizes), width), F32)],
    )(*rows, w_gate, w_up, w_down)


def combine_kernel(count, *refs):
    rows, (target_ref, values_ref, stream_ref, out_ref) = refs[:count], refs[count:]
    returned = jnp.concatenate([r[...] for r in rows], 0)
    total = stream_ref[...]
    for k in range(2):
        pick = (target_ref[:, k : k + 1] == iota((total.shape[0], returned.shape[0]), 1)).astype(F32).astype(BF16)
        total = total + values_ref[:, k : k + 1] * dot(pick, returned)
    out_ref[...] = total.astype(BF16)


def pinned(first, *later):
    return lax.optimization_barrier((first, *later))[1:]


def on_device(
    hidden,
    ssm_input,
    ssm_gate,
    write_proj,
    read_proj,
    dt_raw,
    dt_bias,
    a_log,
    d_skip,
    norm_gain,
    out_weight,
    moe_gain,
    expert_ids,
    gate_values,
    w_gate,
    w_up,
    w_down,
):
    signal, gate, write, read = ssm_input[0], ssm_gate[0], write_proj[0], read_proj[0]
    length, inner = signal.shape
    width = hidden.shape[2]
    heads, state = dt_raw.shape[1], write.shape[1]
    n_seq, n_exp = lax.axis_size("seq"), lax.axis_size("exp")
    experts = n_exp * w_gate.shape[0]
    capacity = max(2, 3 * length // experts)
    slots = experts * capacity
    direct = n_exp == 8 and capacity % 16 == 0 and w_gate.shape[0] == 1
    shape = jax.ShapeDtypeStruct

    cum, step, decay, *states = call(
        state_kernel,
        "block_state",
        [shape((length, heads), F32), shape((length, heads), F32), shape((1, inner), F32)]
        + [shape((state, inner // CHUNKS), BF16)] * CHUNKS,
        2 * length * state * inner,
        2 * length * inner,
    )(dt_raw[0], dt_bias[None], a_log[None], signal, write)

    part = inner // CHUNKS
    incoming = [jnp.zeros_like(s) for s in states]
    received = [lax.ppermute(s, "seq", [(0, 1)]) for s in states]
    for hop in range(2, n_seq):
        for k in range(CHUNKS):
            incoming[k] = incoming[k] + received[k]
            sent = decay[:, k * part : (k + 1) * part] * incoming[k].astype(F32) + states[k].astype(F32)
            sent = lax.optimization_barrier(sent.astype(BF16))
            received[k] = lax.ppermute(sent, "seq", [(hop - 1, hop)])

    own, factor, route, targets = call(
        functools.partial(intra_kernel, direct, capacity),
        "intra_block",
        [
            shape((length, inner), F32),
            shape((length, inner), F32),
            shape((slots, length), BF16),
            shape((length, 2), jnp.int32),
        ],
        4 * length * length * inner,
        12 * length * inner,
    )(cum, step, signal, gate, write, read, d_skip[None], expert_ids[0])

    blocks = [capacity] * n_exp if direct else [slots]
    stream, *buffers = call(
        functools.partial(mix_kernel, CHUNKS),
        "mix",
        [shape((length, width), F32)] + [shape((n, width), BF16) for n in blocks],
        2 * length * inner * width,
        8 * length * inner,
        scratch_shapes=[pltpu.VMEM((length, inner), F32)],
    )(
        *incoming,
        *received,
        read,
        own,
        factor,
        norm_gain[None],
        out_weight,
        hidden[0],
        moe_gain[None],
        route,
    )

    weights = (w_gate[0], w_up[0], w_down[0])
    if direct:
        swap = lambda rows, k: lax.ppermute(rows, "exp", [(i, i ^ k) for i in range(n_exp)])
        arrived, returned = [None] * n_exp, [None] * n_exp
        arrived[0] = buffers[0]
        for k in (6, 7, 4, 5, 2, 3, 1):
            arrived[k] = swap(buffers[k], k)
        for group in ((6, 7), (4, 5), (2, 3), (0, 1)):
            results = run_expert([arrived[k] for k in group], *weights)
            for k, rows in zip(group, results):
                returned[k] = rows if k == 0 else swap(rows, k)
    else:
        trade = lambda rows: lax.all_to_all(
            rows.reshape(n_exp, -1, width), "exp", split_axis=0, concat_axis=0, tiled=True
        ).reshape(-1, width)
        returned = [trade(run_expert([trade(buffers[0])], *weights)[0])]

    total = call(
        functools.partial(combine_kernel, len(returned)),
        "combine",
        shape((length, width), BF16),
        4 * length * slots * width,
        2 * slots * width,
    )(*returned, targets, gate_values[0], stream)
    return total[None]


def solution(mesh):
    in_specs = (
        P("exp", "seq", None),
        P("exp", "seq", None),
        P("exp", "seq", None),
        P("exp", "seq", None),
        P("exp", "seq", None),
        P("exp", None, "seq"),
        P(),
        P(),
        P(),
        P(),
        P(),
        P(),
        P("exp", "seq", None),
        P("exp", "seq", None),
        P("exp", None, None),
        P("exp", None, None),
        P("exp", None, None),
    )
    out_specs = P("exp", "seq", None)
    return jax.shard_map(
        on_device, mesh=mesh, in_specs=in_specs, out_specs=out_specs, check_vma=False
    )
```

```python
import functools

import jax
import jax.numpy as jnp
from jax import lax
from jax.experimental import pallas as pl
from jax.experimental.pallas import tpu as pltpu
from jax.sharding import PartitionSpec as P

EPS = 1e-05
F32 = jnp.float32
BF16 = jnp.bfloat16
CHUNKS = 3
K2_MIB = 32


def call(body, name, out_shape, flops, nbytes, mib=32, **kwargs):
    return pl.pallas_call(
        body,
        out_shape=out_shape,
        name=name,
        compiler_params=pltpu.CompilerParams(vmem_limit_bytes=mib * 2**20),
        cost_estimate=pl.CostEstimate(flops=flops, bytes_accessed=nbytes, transcendentals=0),
        **kwargs,
    )


def dot(a, b):
    return jnp.dot(a, b, preferred_element_type=F32)


def dot_rows(a, b):
    return lax.dot_general(a, b, (((0,), (0,)), ((), ())), preferred_element_type=F32)


def pieces(value, count):
    parts = []
    for _ in range(count):
        part = value.astype(BF16)
        parts.append(part)
        value = value - part.astype(F32)
    return parts


def iota(shape, dim):
    return lax.broadcasted_iota(jnp.int32, shape, dim)


def fetch(sources, buffers, sems):
    copies = [pltpu.make_async_copy(s, b, sems.at[i]) for i, (s, b) in enumerate(zip(sources, buffers))]
    for copy in copies:
        copy.start()
    return copies


def parts_of(ref, count):
    width = ref.shape[1] // count
    return [ref.at[:, k * width : (k + 1) * width] for k in range(count)]


def lead_kernel(*refs):
    @pl.when(lax.axis_index("seq") == 0)
    def _():
        block_state(refs[:5], (), (), refs[5 : 5 + CHUNKS], refs[5 + CHUNKS :])


def state_kernel(*refs):
    block_state(refs[:5], refs[5:7], refs[7 : 7 + CHUNKS], refs[7 + CHUNKS : 7 + 2 * CHUNKS], refs[7 + 2 * CHUNKS :])


def block_state(arrays, step_refs, decay_refs, state_refs, scratch):
    dt_hbm, bias_hbm, alog_hbm, x_hbm, write_hbm = arrays
    dt_ref, bias_ref, alog_ref, x_ref, write_ref, sems = scratch
    length, inner = x_ref.shape
    heads = dt_ref.shape[0]
    copies = fetch(
        [dt_hbm, bias_hbm, alog_hbm, write_hbm] + parts_of(x_hbm, CHUNKS),
        [dt_ref, bias_ref, alog_ref, write_ref] + parts_of(x_ref, CHUNKS),
        sems,
    )
    lower = (iota((length, length), 0) >= iota((length, length), 1)).astype(F32).astype(BF16)
    expand = (iota((heads, inner), 1) // (inner // heads) == iota((heads, inner), 0)).astype(F32).astype(BF16)
    for copy in copies[:3]:
        copy.wait()
    raw = dt_ref[...].T + bias_ref[...]
    step = jnp.maximum(raw, 0.0) + jnp.log1p(jnp.exp(-jnp.abs(raw)))
    log_decay = -jnp.exp(alog_ref[...]) * step
    cum = sum(dot(lower, part) for part in pieces(log_decay, 3))
    last = cum[length - 1 : length, :]
    to_end = jnp.exp(jnp.minimum(last - cum, 0.0)) * step
    if step_refs:
        decay = sum(dot(part, expand) for part in pieces(jnp.broadcast_to(jnp.exp(last), (8, heads)), 3))
        step_refs[0][...] = cum
        step_refs[1][...] = step
    ends = pieces(to_end, 2)
    width = inner // CHUNKS
    copies[3].wait()
    for k in range(CHUNKS):
        cols = slice(k * width, (k + 1) * width)
        if step_refs:
            decay_refs[k][...] = decay[0:1, cols]
        wide = sum(dot(part, expand[:, cols]) for part in ends)
        copies[4 + k].wait()
        scaled = (x_ref[:, cols].astype(F32) * wide).astype(BF16)
        state_refs[k][...] = dot_rows(write_ref[...], scaled).astype(BF16)


def intra_kernel(xor, capacity, cum_ref, step_ref, x_ref, gate_ref, write_ref, read_ref, skip_ref, ids_ref,
                 own_ref, factor_ref, route_ref, target_ref):
    length, inner = x_ref.shape
    experts = route_ref.shape[0] // capacity
    hits = [(ids_ref[k : k + 1, :] == iota((experts, length), 0)).astype(F32) for k in range(2)]
    earlier = (iota((length, length), 0) < iota((length, length), 1)).astype(F32).astype(BF16)
    before = dot((hits[0] + hits[1]).astype(BF16), earlier)
    rows = jnp.zeros(route_ref.shape, F32)
    for k in range(2):
        slot = jnp.sum(before * hits[k], axis=0, keepdims=True).astype(jnp.int32)
        owner = ids_ref[k : k + 1, :]
        if xor:
            owner = owner ^ lax.axis_index("exp")
        target = owner * capacity + slot
        target_ref[k : k + 1, :] = target.astype(F32)
        rows = jnp.where(target == iota(route_ref.shape, 0), 1.0, rows)
    route_ref[...] = rows.astype(BF16)
    heads = cum_ref.shape[1]
    half = length // 2
    cum = cum_ref[...]
    cum_rows = cum.T
    step_rows = step_ref[...].T
    scores = lax.dot_general(
        read_ref[...], write_ref[...], (((1,), (1,)), ((), ())), preferred_element_type=F32
    )
    scores = jnp.where(iota((length, length), 0) >= iota((length, length), 1), scores, 0.0)
    lanes = 2 * (inner // heads)
    first = iota((length, lanes), 1) < lanes // 2
    first_row = iota((1, lanes), 1) < lanes // 2
    for pair in range(heads // 2):
        cols = slice(pair * lanes, (pair + 1) * lanes)
        x = x_ref[:, cols]
        wide = x.astype(F32)
        masked = [jnp.where(first, wide, 0.0).astype(BF16), jnp.where(first, 0.0, wide).astype(BF16)]
        tops, bottoms = [], []
        for h in (2 * pair, 2 * pair + 1):
            here = cum[:, h : h + 1]
            there = cum_rows[h : h + 1, :]
            steps = step_rows[h : h + 1, :]
            top = jnp.exp(jnp.minimum(here[:half] - there[:, :half], 0.0))
            tops.append((scores[:half, :half] * top * steps[:, :half]).astype(BF16))
            bottom = jnp.exp(jnp.minimum(here[half:] - there, 0.0))
            bottoms.append((scores[half:, :] * bottom * steps).astype(BF16))
        y_top = dot(jnp.concatenate(tops, 1), jnp.concatenate([m[:half] for m in masked], 0))
        y_bottom = dot(jnp.concatenate(bottoms, 1), jnp.concatenate(masked, 0))
        y = jnp.concatenate([y_top, y_bottom], 0)
        skip = jnp.where(first_row, skip_ref[:, 2 * pair : 2 * pair + 1], skip_ref[:, 2 * pair + 1 : 2 * pair + 2])
        gate = gate_ref[:, cols].astype(F32)
        gate = gate / (1.0 + jnp.exp(-gate))
        grown = jnp.exp(jnp.where(first, cum[:, 2 * pair : 2 * pair + 1], cum[:, 2 * pair + 1 : 2 * pair + 2]))
        own_ref[:, cols] = ((y + skip * wide) * gate).astype(own_ref.dtype)
        factor_ref[:, cols] = (grown * gate).astype(factor_ref.dtype)


def mix_kernel(chunks, *refs):
    earlier, latest = refs[:chunks], refs[chunks : 2 * chunks]
    (read_ref, own_ref, factor_ref, norm_ref, weight_ref, hidden_ref, gain_ref, route_ref) = refs[2 * chunks : 2 * chunks + 8]
    stream_ref, *buffer_refs, mixed_ref = refs[2 * chunks + 8 :]
    inner = own_ref.shape[1]
    width = inner // chunks
    total = 0.0
    for k in range(chunks):
        cols = slice(k * width, (k + 1) * width)
        incoming = (earlier[k][...].astype(F32) + latest[k][...].astype(F32)).astype(BF16)
        value = own_ref[:, cols] + factor_ref[:, cols] * dot(read_ref[...], incoming)
        mixed_ref[:, cols] = value
        total = total + jnp.sum(value * value, axis=1, keepdims=True)
    scale = lax.rsqrt(total / inner + EPS)
    gated = (mixed_ref[...] * scale * norm_ref[...]).astype(BF16)
    stream = hidden_ref[...].astype(F32) + dot(gated, weight_ref[...])
    stream_ref[...] = stream
    scale = lax.rsqrt(jnp.mean(stream * stream, axis=1, keepdims=True) + EPS)
    normed = (stream * scale * gain_ref[...]).astype(BF16)
    at = 0
    for buffer_ref in buffer_refs:
        rows = buffer_ref.shape[0]
        buffer_ref[...] = dot(route_ref[at : at + rows, :], normed).astype(BF16)
        at += rows


def expert_kernel(count, *refs):
    rows, (gate_ref, up_ref, down_ref), outs = refs[:count], refs[count : count + 3], refs[count + 3 :]
    x = jnp.concatenate([r[...] for r in rows], 0)
    hidden = gate_ref.shape[1]
    tile = hidden // 3
    total = 0.0
    for k in range(3):
        cols = slice(k * tile, (k + 1) * tile)
        gate = dot(x, gate_ref[:, cols])
        active = (gate / (1.0 + jnp.exp(-gate)) * dot(x, up_ref[:, cols])).astype(BF16)
        total = total + dot(active, down_ref[cols, :])
    at = 0
    for out in outs:
        out[...] = total[at : at + out.shape[0], :].astype(BF16)
        at += out.shape[0]


def run_expert(rows, w_gate, w_up, w_down):
    width = w_gate.shape[0]
    sizes = [r.shape[0] for r in rows]
    return call(
        functools.partial(expert_kernel, len(rows)),
        "experts",
        [jax.ShapeDtypeStruct((n, width), BF16) for n in sizes],
        sum(sizes),
        sum(sizes),
    )(*rows, w_gate, w_up, w_down)


def combine_kernel(order, *refs):
    count = len(order)
    rows, (target_ref, values_ref, stream_ref, out_ref) = refs[:count], refs[count:]
    returned = jnp.concatenate([rows[order.index(k)][...] for k in range(count)], 0)
    total = stream_ref[...]
    length = total.shape[0]
    columns = jnp.concatenate([target_ref[...], values_ref[...], jnp.zeros((4, length), F32)], 0).T
    for k in range(2):
        target = columns[:, k : k + 1].astype(jnp.int32)
        pick = (target == iota((length, returned.shape[0]), 1)).astype(F32).astype(BF16)
        total = total + columns[:, 2 + k : 3 + k] * dot(pick, returned)
    out_ref[...] = total.astype(BF16)


def on_device(
    hidden,
    ssm_input,
    ssm_gate,
    write_proj,
    read_proj,
    dt_raw,
    dt_bias,
    a_log,
    d_skip,
    norm_gain,
    out_weight,
    moe_gain,
    expert_ids,
    gate_values,
    w_gate,
    w_up,
    w_down,
):
    signal, gate, write, read = ssm_input[0], ssm_gate[0], write_proj[0], read_proj[0]
    length, inner = signal.shape
    width = hidden.shape[2]
    heads, state = dt_raw.shape[1], write.shape[1]
    n_seq, n_exp = lax.axis_size("seq"), lax.axis_size("exp")
    experts = n_exp * w_gate.shape[0]
    capacity = max(2, 3 * length // experts)
    slots = experts * capacity
    direct = n_exp == 8 and capacity % 16 == 0 and w_gate.shape[0] == 1
    shape = jax.ShapeDtypeStruct

    part = inner // CHUNKS
    operands = (dt_raw[0], dt_bias[None], a_log[None], signal, write)
    state_shapes = [shape((state, part), BF16)] * CHUNKS
    state_call = dict(
        mib=60,
        in_specs=[pl.BlockSpec(memory_space=pltpu.HBM)] * 5,
        scratch_shapes=[
            pltpu.VMEM((heads, length), F32),
            pltpu.VMEM((1, heads), F32),
            pltpu.VMEM((1, heads), F32),
            pltpu.VMEM((length, inner), BF16),
            pltpu.VMEM((length, state), BF16),
            pltpu.SemaphoreType.DMA((4 + CHUNKS,)),
        ],
    )
    work = (2 * length * state * inner, 2 * length * inner)
    lead = call(lead_kernel, "first_state", state_shapes, *work, **state_call)(*operands)
    received = [lax.ppermute(s, "seq", [(0, 1)]) for s in lead]
    dt_own, _ = lax.optimization_barrier((dt_raw[0], lead[0]))
    cum, step, *chain = call(
        state_kernel,
        "block_state",
        [shape((length, heads), F32)] * 2 + [shape((1, part), F32)] * CHUNKS + state_shapes,
        *work,
        **state_call,
    )(dt_own, *operands[1:])

    decays, states = chain[:CHUNKS], chain[CHUNKS:]
    incoming = [jnp.zeros_like(s) for s in states]
    received[0], cum = lax.optimization_barrier((received[0], cum))
    def intra(cum):
        return call(
            functools.partial(intra_kernel, direct, capacity),
            "intra_block",
            [
                shape((length, inner), F32),
                shape((length, inner), F32),
                shape((slots, length), BF16),
                shape((2, length), F32),
            ],
            4 * length * length * inner,
            12 * length * inner,
            mib=K2_MIB,
        )(cum, step, signal, gate, write, read, d_skip[None], expert_ids[0].T)

    for hop in range(2, n_seq):
        for k in range(CHUNKS):
            incoming[k] = incoming[k] + received[k] if hop > 2 else received[k]
            sent = decays[k] * incoming[k].astype(F32) + states[k].astype(F32)
            sent, incoming[k] = lax.optimization_barrier((sent.astype(BF16), incoming[k]))
            received[k] = lax.ppermute(sent, "seq", [(hop - 1, hop)])
        if hop == 2:
            cum, sent = lax.optimization_barrier((cum, sent))
            own, factor, route, targets = intra(cum)
            received[0], own = lax.optimization_barrier((received[0], own))

    blocks = [capacity] * n_exp if direct else [slots]
    stream, *buffers = call(
        functools.partial(mix_kernel, CHUNKS),
        "mix",
        [shape((length, width), F32)] + [shape((n, width), BF16) for n in blocks],
        2 * length * inner * width,
        8 * length * inner,
        scratch_shapes=[pltpu.VMEM((length, inner), F32)],
    )(
        *incoming,
        *received,
        read,
        own,
        factor,
        norm_gain[None],
        out_weight,
        hidden[0],
        moe_gain[None],
        route,
    )

    weights = (w_gate[0], w_up[0], w_down[0])
    if direct:
        swap = lambda rows, k: lax.ppermute(rows, "exp", [(i, i ^ k) for i in range(n_exp)])
        arrived = [buffers[0]] + [None] * (n_exp - 1)
        returned = [None] * n_exp
        for k in (1, 6, 7, 2, 4, 3, 5):
            arrived[k] = swap(buffers[k], k)
        before = None
        groups = ((0, 1), (6, 7), (2, 4), (3, 5))
        order = [k for group in groups for k in group]
        for group in groups:
            rows = [arrived[k] for k in group]
            if before is not None:
                *rows, before = lax.optimization_barrier((*rows, before))
            results = run_expert(rows, *weights)
            before = results[0]
            for k, rows in zip(group, results):
                returned[k] = rows if k == 0 else swap(rows, k)
    else:
        trade = lambda rows: lax.all_to_all(
            rows.reshape(n_exp, -1, width), "exp", split_axis=0, concat_axis=0, tiled=True
        ).reshape(-1, width)
        order = [0]
        returned = [trade(run_expert([trade(buffers[0])], *weights)[0])]

    total = call(
        functools.partial(combine_kernel, order),
        "combine",
        shape((length, width), BF16),
        4 * length * slots * width,
        2 * slots * width,
    )(*[returned[k] for k in order], targets, gate_values[0].T, stream)
    return total[None]


def solution(mesh):
    in_specs = (
        P("exp", "seq", None),
        P("exp", "seq", None),
        P("exp", "seq", None),
        P("exp", "seq", None),
        P("exp", "seq", None),
        P("exp", None, "seq"),
        P(),
        P(),
        P(),
        P(),
        P(),
        P(),
        P("exp", "seq", None),
        P("exp", "seq", None),
        P("exp", None, None),
        P("exp", None, None),
        P("exp", None, None),
    )
    out_specs = P("exp", "seq", None)
    return jax.shard_map(
        on_device, mesh=mesh, in_specs=in_specs, out_specs=out_specs, check_vma=False
    )
```
